512 devices in a mesh: orb: 64 (over z_hi, x, y), dom: 8 (over z_lo, core).
Axes of the slice: x: 4, y: 4, z: 16 (z_hi: 4, z_lo: 4; z = z_hi * 4 + z_lo), core: 2. Of those that a mesh axis runs over, the one named last changes fastest.
Arguments:
- orbitals: float32 [64, 2, 96, 128, 128], P('orb', None, 'dom'), may hold values from -7 to 7, as said below
- occupations: float32 [64], P('orb'), may hold values from 0.5 to 2
- potential: float32 [96, 128, 128], P('dom'), may hold values from -4 to 4
Outputs:
- new_orbitals: float32 [64, 2, 96, 128, 128], P('orb', None, 'dom')
- hartree: float32 [96, 128, 128], P('dom', 'orb')
The draws below stay inside these ranges and needn't reach their ends.
Inputs may be any that keep to these rules, and one draw needn't show every extreme that they name: `orbitals`: real and imaginary parts of order one.
All inputs are finite; a program needn't handle non-finite values.
Results may differ from the reference program's by a relative error of at most 0.0018.
Values sent between devices are 32-bit elements; how exact they have to be, the bound alone decides.
A program may use at most 64 MiB of HBM per device.

```python
import math
import jax
import jax.numpy as jnp
from jax import lax

NX = 96
NY = 128
NZ = 128
TERMS = 4
ORBS = 64


def draw_orbitals(key, part):
    key = jax.random.fold_in(key, 11)
    shape = (ORBS, 2, NX, NY, NZ)
    base = jnp.clip(jax.random.normal(key, shape, jnp.float32), -6.0, 6.0)
    depth = 0.1
    parity = (jnp.arange(NY, dtype=jnp.int32)[:, None] + jnp.arange(NZ, dtype=jnp.int32)[None, :]) % 2
    factor = 1.0 + depth * (1.0 - 2.0 * parity.astype(jnp.float32))
    return (base * factor).astype(jnp.float32)


def levels(own_key, dims, pieces, least, largest):
    def one(position, shards_of):
        draws = jax.random.uniform(jax.random.fold_in(jax.random.fold_in(own_key, 6), position), (shards_of,), jnp.float32, least / len(pieces), largest / len(pieces))
        return jnp.repeat(jnp.exp(draws), dims[position] // shards_of).reshape((-1,) + (1,) * (len(dims) - position - 1))

    gain = one(*pieces[0])
    for cut in pieces[1:]:
        gain = gain * one(*cut)
    return gain


def setup_inputs(seed: int = 0) -> dict:
    streams_of = jax.random.split(jax.random.key(seed), 4)
    orbitals = draw_orbitals(jax.random.fold_in(streams_of[3], 71), 0)
    occupations = jnp.clip(jnp.exp(math.log(2.0) - 1.3862944 * jax.random.uniform(streams_of[1], (ORBS,), jnp.float32) ** levels(streams_of[1], (ORBS,), ((0, 64),), -0.2, 0.2)), 0.5, 2.0)
    potential = jnp.clip(jax.random.uniform(streams_of[2], (NX, NY, NZ), jnp.float32, -4.0, 4.0) * levels(streams_of[2], (NX, NY, NZ), ((0, 8),), -0.4, 0.0), -4.0, 4.0)
    return {"orbitals": orbitals, "occupations": occupations, "potential": potential}


SPACING = 0.4
TIME_STEP = 0.03
STENCIL = (-205.0 / 72.0, 8.0 / 5.0, -1.0 / 5.0, 8.0 / 315.0, -1.0 / 560.0)

def laplacian_rows(padded):
    rows = padded.shape[2] - 8
    across = padded.shape[3]
    along = padded.shape[4]
    full = jnp.pad(padded, ((0, 0), (0, 0), (0, 0), (4, 4), (4, 4)))
    total = 3.0 * STENCIL[0] * full[:, :, 4:4 + rows, 4:4 + across, 4:4 + along]
    for reach in range(1, 5):
        pairs = full[:, :, 4 + reach:4 + reach + rows, 4:4 + across, 4:4 + along] + full[:, :, 4 - reach:4 - reach + rows, 4:4 + across, 4:4 + along]
        pairs = pairs + full[:, :, 4:4 + rows, 4 + reach:4 + reach + across, 4:4 + along] + full[:, :, 4:4 + rows, 4 - reach:4 - reach + across, 4:4 + along]
        pairs = pairs + full[:, :, 4:4 + rows, 4:4 + across, 4 + reach:4 + reach + along] + full[:, :, 4:4 + rows, 4:4 + across, 4 - reach:4 - reach + along]
        total = total + STENCIL[reach] * pairs
    return total / (SPACING * SPACING)

def next_term(padded, potential_rows, order):
    rows = padded.shape[2] - 8
    center = padded[:, :, 4:4 + rows]
    applied = -0.5 * laplacian_rows(padded) + potential_rows * center
    return TIME_STEP / order * jnp.stack([applied[:, 1], -applied[:, 0]], axis=1)

def wave_squares(index, length):
    signed = jnp.minimum(index, length - index).astype(jnp.float32)
    scaled = signed * (2.0 * math.pi / (length * SPACING))
    return scaled * scaled

def reference(orbitals, occupations, potential):
    potential_full = potential[None, None]

    def advance(density, inputs):
        orbital, weight = inputs
        term = orbital[None]
        result = term
        for order in range(1, TERMS):
            padded = jnp.pad(term, ((0, 0), (0, 0), (4, 4), (0, 0), (0, 0)))
            term = next_term(padded, potential_full, order)
            result = result + term
        moved = result[0]
        density = density + weight * (moved[0] * moved[0] + moved[1] * moved[1])
        return (density, moved)
    start = jnp.zeros((NX, NY, NZ), jnp.float32)
    density, moved_all = lax.scan(advance, start, (orbitals, occupations))
    density = density / math.sqrt(ORBS)
    wave_x = wave_squares(jnp.arange(NX, dtype=jnp.int32), NX)
    wave_y = wave_squares(jnp.arange(NY, dtype=jnp.int32), NY)
    wave_z = wave_squares(jnp.arange(NZ, dtype=jnp.int32), NZ)
    squares = wave_x[:, None, None] + wave_y[None, :, None] + wave_z[None, None, :]
    kernel = jnp.where(squares > 0.0, 4.0 * math.pi / jnp.where(squares > 0.0, squares, 1.0), 0.0)
    modes = jnp.fft.fftn(density)
    hartree = jnp.real(jnp.fft.ifftn(modes * kernel)).astype(jnp.float32)
    return (moved_all, hartree)
```

```python
import functools
import math

import jax
import jax.numpy as jnp
import numpy as np
from jax import lax
from jax.experimental import pallas as pl
from jax.experimental.pallas import tpu as pltpu
from jax.sharding import PartitionSpec as P

MESH = pl.DeviceIdType.MESH
HIGHEST = lax.Precision.HIGHEST
SPACING = 0.4
TIME_STEP = 0.03
STENCIL = (-205.0 / 72.0, 8.0 / 5.0, -1.0 / 5.0, 8.0 / 315.0, -1.0 / 560.0)
COEF = tuple(-0.5 * c / (SPACING * SPACING) for c in STENCIL)


def real_basis(n):
    grid = np.arange(n)
    rows = np.zeros((n, n))
    for k in range(n):
        m = (k + 1) // 2
        angle = 2.0 * np.pi * ((m * grid) % n) / n
        wave = np.cos(angle) if (k % 2 == 1 or k == 0) else np.sin(angle)
        rows[k] = wave * (np.sqrt(1.0 / n) if m in (0, n // 2) else np.sqrt(2.0 / n))
    return rows


def band(n):
    out = np.zeros((n, n))
    for r in range(1, 5):
        out += COEF[r] * (np.eye(n, k=r) + np.eye(n, k=-r))
    return out


def squares_of(n):
    m = (np.arange(n) + 1) // 2
    return (m * (2.0 * math.pi / (n * SPACING))) ** 2


def dot(a, b):
    return jnp.dot(a, b, precision=HIGHEST, preferred_element_type=jnp.float32)


def orbitals_kernel(dims, occ_ref, orb_ref, pot_ref, dz_ref, dy_ref, new_ref, rho_ref, buf, send, recv, load):
    doms, planes, total_orbs = dims
    last = 4 + planes
    d = lax.axis_index("dom")
    odd = lax.rem(d, 2)
    fast_id = d + 1 - 2 * odd
    slow_id = d - 1 + 2 * odd
    has_slow = jnp.logical_and(slow_id >= 0, slow_id < doms)
    base_fast = (1 - odd) * (planes - 4)
    base_slow = odd * (planes - 4)

    barrier = pltpu.get_barrier_semaphore()
    pl.semaphore_signal(barrier, inc=1, device_id={"dom": fast_id}, device_id_type=MESH)

    @pl.when(has_slow)
    def _():
        pl.semaphore_signal(barrier, inc=1, device_id={"dom": slow_id}, device_id_type=MESH)

    loads = [
        pltpu.make_async_copy(orb_ref.at[0, c], buf.at[0, c, pl.ds(4, planes)], load.at[c]) for c in range(2)
    ]
    for copy in loads:
        copy.start()

    @pl.when(has_slow)
    def _():
        pl.semaphore_wait(barrier, 2)

    @pl.when(jnp.logical_not(has_slow))
    def _():
        pl.semaphore_wait(barrier, 1)

    def halo(k, c, side):
        base = base_slow if side else base_fast
        dst = jnp.where(odd == (0 if side else 1), last, 0)
        if k == 0:
            src = orb_ref.at[0, c, pl.ds(base, 4)]
        else:
            src = buf.at[k, c, pl.ds(4 + base, 4)]
        return pltpu.make_async_remote_copy(
            src_ref=src,
            dst_ref=buf.at[k, c, pl.ds(dst, 4)],
            send_sem=send.at[k, c, side],
            recv_sem=recv.at[k, c, side],
            device_id={"dom": slow_id if side else fast_id},
            device_id_type=MESH,
        )

    def start(k, c, side):
        if side:

            @pl.when(has_slow)
            def _():
                halo(k, c, side).start()

        else:
            halo(k, c, side).start()

    def arrived(k, c, side):
        if side:

            @pl.when(has_slow)
            def _():
                halo(k, c, side).wait_recv()

        else:
            halo(k, c, side).wait_recv()

    for c in range(2):
        start(0, c, 1)
        start(0, c, 0)

    @pl.when(jnp.logical_not(has_slow))
    def _():
        edge = odd * last
        for k in range(3):
            for c in range(2):
                buf[k, c, pl.ds(edge, 4)] = jnp.zeros((4,) + buf.shape[3:], jnp.float32)

    def step(k, c, x):
        f = buf[k, c, 4 + x]
        high = f.astype(jnp.bfloat16)
        low = (f - high.astype(jnp.float32)).astype(jnp.bfloat16)
        h = jnp.dot(jnp.concatenate([high, low], axis=1), dz_ref[...], preferred_element_type=jnp.float32)
        h = h + jnp.dot(dy_ref[...], jnp.concatenate([high, low], axis=0), preferred_element_type=jnp.float32)
        h = h + (3.0 * COEF[0] + pot_ref[x]) * f
        for r in range(1, 5):
            h = h + COEF[r] * (buf[k, c, 4 + x + r] + buf[k, c, 4 + x - r])
        sign = 1.0 if (k + c) % 2 else -1.0
        return (sign * TIME_STEP / (k + 1)) * h

    weight = occ_ref[0] * (1.0 / math.sqrt(total_orbs))

    def sweep(k, c, base, count):
        def body(i, carry):
            x = base + i
            out = step(k, c, x)
            if k < 2:
                buf[k + 1, c, 4 + x] = out
            elif c == 0:
                new_ref[0, 1, x] = ((buf[0, 1, 4 + x] + buf[1, 0, 4 + x]) + buf[2, 1, 4 + x]) + out
            else:
                real = ((buf[0, 0, 4 + x] + buf[1, 1, 4 + x]) + buf[2, 0, 4 + x]) + out
                new_ref[0, 0, x] = real
                imag = new_ref[0, 1, x]
                rho_ref[x] = weight * (real * real + imag * imag)
            return carry

        lax.fori_loop(0, count, body, 0)

    def edges(k, c):
        for side in range(2):
            arrived(k, c, side)
            sweep(k, c, base_slow if side else base_fast, 4)
            if k < 2:
                start(k + 1, c, side)

    for c in range(2):
        loads[c].wait()
        sweep(0, c, 4, planes - 8)
    edges(0, 0)
    sweep(1, 0, 4, planes - 8)
    edges(0, 1)
    sweep(1, 1, 4, planes - 8)
    edges(1, 0)
    edges(1, 1)
    sweep(2, 0, 4, planes - 8)
    sweep(2, 1, 4, planes - 8)
    edges(2, 0)
    edges(2, 1)
    for k in range(3):
        for c in range(2):
            halo(k, c, 0).wait_send()

            @pl.when(has_slow)
            def _():
                halo(k, c, 1).wait_send()


def hartree_kernel(
    dims,
    rho_ref,
    wy_ref,
    iy_ref,
    rz_ref,
    rzt_ref,
    rx_ref,
    rxt_ref,
    qx_ref,
    qz_ref,
    out_ref,
    m1,
    r1,
    s1,
    r2,
    s2,
    r3,
    xs,
    y3,
    r4,
    m5,
    r5,
    s5,
    r6,
    send1,
    recv1,
    send2,
    recv2,
    send3,
    recv3,
    send4,
    recv4,
    send5,
    recv5,
    send6,
    recv6,
):
    A, B, C, D, planes, ny, nz = dims
    half = planes // 2
    groups = B * C
    keep = ny // groups
    rows_a = ny // A
    rows_own = ny // (A * groups)
    line = A * D
    stride = line // keep
    orb = lax.axis_index("orb")
    dom = lax.axis_index("dom")
    a = orb // groups
    b = lax.rem(orb // C, B)
    c = lax.rem(orb, C)
    me = a * D + dom

    def along(axis, offset):
        if axis == 0:
            return a * groups + lax.rem(b + offset, B) * C + c
        return a * groups + b * C + lax.rem(c + offset, C)

    def on_line(place):
        return (place // D) * groups + b * C + c, lax.rem(place, D)

    size = (B, C)
    mine = (b, c)
    barrier = pltpu.get_barrier_semaphore()
    for axis in range(2):
        for o in range(1, size[axis]):
            pl.semaphore_signal(barrier, inc=1, device_id={"orb": along(axis, o)}, device_id_type=MESH)

    def greet(o, carry):
        place = on_line(lax.rem(me + o, line))
        pl.semaphore_signal(barrier, inc=1, device_id={"orb": place[0], "dom": place[1]}, device_id_type=MESH)
        return carry

    lax.fori_loop(1, line, greet, 0)

    def forward(x, carry):
        m1[x] = dot(wy_ref[0], rho_ref[x])
        m1[half + x] = dot(wy_ref[1], rho_ref[half + x])
        return carry

    lax.fori_loop(0, half, forward, 0)
    pl.semaphore_wait(barrier, B - 1 + C - 1 + line - 1)

    def exchange(src, dst, sends, recvs, h, axis, o, count, pre):
        peer = lax.rem(mine[axis] + o, size[axis])
        return pltpu.make_async_remote_copy(
            src_ref=src(peer),
            dst_ref=dst,
            send_sem=sends.at[h, o - 1],
            recv_sem=recvs.at[h, o - 1],
            device_id={"orb": along(axis, o)},
            device_id_type=MESH,
        )

    copies1 = []
    for h in range(2):
        axis = h
        big = ny // size[axis]
        for o in range(1, size[axis]):
            copies1.append(
                exchange(
                    lambda p, h=h, big=big: m1.at[pl.ds(h * half, half), pl.ds(pl.multiple_of(p * big, 8), big)],
                    r1.at[h, o - 1],
                    send1,
                    recv1,
                    h,
                    axis,
                    o,
                    None,
                    None,
                )
            )
    for copy in copies1:
        copy.start()
    copies2 = []
    at = 0
    for h in range(2):
        axis = h
        big = ny // size[axis]
        own = pl.ds(pl.multiple_of(mine[axis] * big, 8), big)
        total = m1[h * half : (h + 1) * half, own]
        for o in range(1, size[axis]):
            copies1[at].wait_recv()
            at += 1
            total = total + r1[h, o - 1]
        s1[h] = total
        other = 1 - h
        for o in range(1, size[other]):
            copy = exchange(
                lambda p, h=h: s1.at[h, :, pl.ds(pl.multiple_of(p * keep, 8), keep)],
                r2.at[h, o - 1],
                send2,
                recv2,
                h,
                other,
                o,
                None,
                None,
            )
            copy.start()
            copies2.append(copy)
    at = 0
    for h in range(2):
        other = 1 - h
        own = pl.ds(pl.multiple_of(mine[other] * keep, 8), keep)
        total = s1[h, :, own]
        for o in range(1, size[other]):
            copies2[at].wait_recv()
            at += 1
            total = total + r2[h, o - 1]
        for x in range(half):
            s2[:, h * half + x, :] = total[x]

    def to_solver(j):
        place = on_line(j * stride)
        return pltpu.make_async_remote_copy(
            src_ref=s2.at[j],
            dst_ref=r3.at[me],
            send_sem=send3.at[j],
            recv_sem=recv3.at[me],
            device_id={"orb": place[0], "dom": place[1]},
            device_id_type=MESH,
        )

    for j in range(keep):

        @pl.when(me != j * stride)
        def _():
            to_solver(j).start()

        @pl.when(me == j * stride)
        def _():
            r3[me] = s2[j]

    def to_slab(place):
        where = on_line(place)
        slab = lax.rem(place, D)
        return pltpu.make_async_remote_copy(
            src_ref=y3.at[slab],
            dst_ref=r4.at[me // stride],
            send_sem=send4.at[place],
            recv_sem=recv4.at[me // stride],
            device_id={"orb": where[0], "dom": where[1]},
            device_id_type=MESH,
        )

    def from_line(place):
        where = on_line(place)
        return pltpu.make_async_remote_copy(
            src_ref=s2.at[0],
            dst_ref=r3.at[place],
            send_sem=send3.at[0],
            recv_sem=recv3.at[place],
            device_id={"orb": where[0], "dom": where[1]},
            device_id_type=MESH,
        )

    @pl.when(lax.rem(me, stride) == 0)
    def _():
        def landed(o, carry):
            from_line(lax.rem(me + o, line)).wait_recv()
            return carry

        lax.fori_loop(1, line, landed, 0)
        for slab in range(D):
            piece = r3[slab]
            for q in range(1, A):
                piece = piece + r3[q * D + slab]
            xs[slab * planes : (slab + 1) * planes, :] = piece
        modes = dot(rx_ref[...], dot(xs[...], rzt_ref[...]))
        wave = (b * C + c) * keep + me // stride
        m = ((wave + 1) // 2).astype(jnp.float32) * (2.0 * math.pi / (ny * SPACING))
        squares = (qx_ref[...] + m * m) + qz_ref[...]
        positive = squares > 0.0
        solved = modes * jnp.where(positive, 4.0 * math.pi / jnp.where(positive, squares, 1.0), 0.0)
        xs[...] = dot(dot(rxt_ref[...], solved), rz_ref[...])
        for slab in range(D):
            y3[slab] = xs[slab * planes : (slab + 1) * planes, :]
        r4[me // stride] = y3[dom]

        def give(o, carry):
            to_slab(lax.rem(me + o, line)).start()
            return carry

        lax.fori_loop(1, line, give, 0)

    def from_solver(j):
        where = on_line(j * stride)
        return pltpu.make_async_remote_copy(
            src_ref=y3.at[0],
            dst_ref=r4.at[j],
            send_sem=send4.at[0],
            recv_sem=recv4.at[j],
            device_id={"orb": where[0], "dom": where[1]},
            device_id_type=MESH,
        )

    for j in range(keep):

        @pl.when(me != j * stride)
        def _():
            from_solver(j).wait_recv()

    first = pl.ds(pl.multiple_of((b * C + c) * keep, 8), keep)
    for h in range(2):
        table = iy_ref[h, first, :]
        for x in range(half):
            rows = r4[:, h * half + x, :]
            m5[h * half + x] = lax.dot_general(
                table, rows, (((0,), (0,)), ((), ())), precision=HIGHEST, preferred_element_type=jnp.float32
            )

    copies5 = []
    for h in range(2):
        axis = h
        big = rows_a // size[axis]
        for o in range(1, size[axis]):
            copy = exchange(
                lambda p, h=h, big=big: m5.at[
                    pl.ds(h * half, half), pl.ds(pl.multiple_of(a * rows_a + p * big, 8), big)
                ],
                r5.at[h, o - 1],
                send5,
                recv5,
                h,
                axis,
                o,
                None,
                None,
            )
            copy.start()
            copies5.append(copy)
    copies6 = []
    at = 0
    for h in range(2):
        axis = h
        other = 1 - h
        big = rows_a // size[axis]
        total = m5[h * half : (h + 1) * half, pl.ds(pl.multiple_of(a * rows_a + mine[axis] * big, 8), big)]
        for o in range(1, size[axis]):
            copies5[at].wait_recv()
            at += 1
            total = total + r5[h, o - 1]
        for p in range(size[other]):
            s5[h, p] = total[:, p * rows_own : (p + 1) * rows_own]
        for o in range(1, size[other]):
            copy = exchange(lambda p, h=h: s5.at[h, p], r6.at[h, o - 1], send6, recv6, h, other, o, None, None)
            copy.start()
            copies6.append(copy)
    at = 0
    for h in range(2):
        other = 1 - h
        total = s5[h, mine[other]]
        for o in range(1, size[other]):
            copies6[at].wait_recv()
            at += 1
            total = total + r6[h, o - 1]
        out_ref[h * half : (h + 1) * half] = total

    for copy in copies1 + copies2 + copies5 + copies6:
        copy.wait_send()
    for j in range(keep):

        @pl.when(me != j * stride)
        def _():
            to_solver(j).wait_send()

    @pl.when(lax.rem(me, stride) == 0)
    def _():
        def gone(o, carry):
            to_slab(lax.rem(me + o, line)).wait_send()
            return carry

        lax.fori_loop(1, line, gone, 0)


def factors(orbs):
    return {64: (4, 4, 4), 8: (2, 2, 2)}[orbs]


def body(orbitals, occupations, potential):
    groups = lax.axis_size("orb")
    doms = lax.axis_size("dom")
    A, B, C = factors(groups)
    planes, ny, nz = potential.shape
    nx = planes * doms
    half = planes // 2
    f32 = jnp.float32
    vmem = pl.BlockSpec(memory_space=pltpu.VMEM)
    dma = pltpu.SemaphoreType.DMA

    dz = band(nz)
    dy = band(ny)
    new, rho = pl.pallas_call(
        functools.partial(orbitals_kernel, (doms, planes, orbitals.shape[0] * groups)),
        out_shape=(jax.ShapeDtypeStruct(orbitals.shape, f32), jax.ShapeDtypeStruct(potential.shape, f32)),
        in_specs=[pl.BlockSpec(memory_space=pltpu.SMEM), pl.BlockSpec(memory_space=pl.ANY), vmem, vmem, vmem],
        out_specs=(vmem, vmem),
        scratch_shapes=[
            pltpu.VMEM((3, 2, planes + 8, ny, nz), f32),
            dma((3, 2, 2)),
            dma((3, 2, 2)),
            dma((2,)),
        ],
        compiler_params=pltpu.CompilerParams(
            collective_id=0, has_side_effects=True, vmem_limit_bytes=40 * 2**20
        ),
    )(
        occupations,
        orbitals,
        potential,
        jnp.asarray(np.concatenate([dz, dz], axis=0), jnp.bfloat16),
        jnp.asarray(np.concatenate([dy, dy], axis=1), jnp.bfloat16),
    )

    ry = real_basis(ny)
    rz = real_basis(nz)
    rx = real_basis(nx)
    keep = ny // (B * C)
    rows_own = ny // groups
    swapped = ry.reshape(B, C, keep, ny).transpose(1, 0, 2, 3).reshape(ny, ny)
    back = ry.reshape(ny, A, B, C, rows_own).transpose(0, 1, 3, 2, 4).reshape(ny, ny)
    dims = (A, B, C, doms, planes, ny, nz)
    line = A * doms
    scratch = [
        pltpu.VMEM((planes, ny, nz), f32),
        pltpu.VMEM((2, B - 1, half, ny // B, nz), f32),
        pltpu.VMEM((2, half, ny // B, nz), f32),
        pltpu.VMEM((2, B - 1, half, keep, nz), f32),
        pltpu.VMEM((keep, planes, nz), f32),
        pltpu.VMEM((line, planes, nz), f32),
        pltpu.VMEM((nx, nz), f32),
        pltpu.VMEM((doms, planes, nz), f32),
        pltpu.VMEM((keep, planes, nz), f32),
        pltpu.VMEM((planes, ny, nz), f32),
        pltpu.VMEM((2, B - 1, half, ny // (A * B), nz), f32),
        pltpu.VMEM((2, B, half, rows_own, nz), f32),
        pltpu.VMEM((2, B - 1, half, rows_own, nz), f32),
        dma((2, B - 1)),
        dma((2, B - 1)),
        dma((2, B - 1)),
        dma((2, B - 1)),
        dma((keep,)),
        dma((line,)),
        dma((line,)),
        dma((keep,)),
        dma((2, B - 1)),
        dma((2, B - 1)),
        dma((2, B - 1)),
        dma((2, B - 1)),
    ]
    tables = [
        np.stack([ry, swapped]),
        np.stack([ry, back]),
        rz,
        rz.T,
        rx,
        rx.T,
        squares_of(nx)[:, None] * np.ones((1, nz)),
        squares_of(nz)[None, :],
    ]
    hartree = pl.pallas_call(
        functools.partial(hartree_kernel, dims),
        out_shape=jax.ShapeDtypeStruct((planes, rows_own, nz), f32),
        in_specs=[vmem] * 9,
        out_specs=vmem,
        scratch_shapes=scratch,
        compiler_params=pltpu.CompilerParams(
            collective_id=1, has_side_effects=True, vmem_limit_bytes=40 * 2**20
        ),
    )(rho, *[jnp.asarray(t, f32) for t in tables])
    return (new, hartree)


def solution(mesh):
    return jax.shard_map(
        body,
        mesh=mesh,
        in_specs=(P("orb", None, "dom", None, None), P("orb"), P("dom", None, None)),
        out_specs=(P("orb", None, "dom", None, None), P("dom", "orb", None)),
        check_vma=False,
    )
```

```python
import functools
import math

import jax
import jax.numpy as jnp
import numpy as np
from jax import lax
from jax.experimental import pallas as pl
from jax.experimental.pallas import tpu as pltpu
from jax.sharding import PartitionSpec as P

MESH = pl.DeviceIdType.MESH
HIGHEST = lax.Precision.HIGHEST
SPACING = 0.4
TIME_STEP = 0.03
STENCIL = (-205.0 / 72.0, 8.0 / 5.0, -1.0 / 5.0, 8.0 / 315.0, -1.0 / 560.0)
COEF = tuple(-0.5 * c / (SPACING * SPACING) for c in STENCIL)


def real_basis(n):
    grid = np.arange(n)
    rows = np.zeros((n, n))
    for k in range(n):
        m = (k + 1) // 2
        angle = 2.0 * np.pi * ((m * grid) % n) / n
        wave = np.cos(angle) if (k % 2 == 1 or k == 0) else np.sin(angle)
        rows[k] = wave * (np.sqrt(1.0 / n) if m in (0, n // 2) else np.sqrt(2.0 / n))
    return rows


def band(n):
    out = np.zeros((n, n))
    for r in range(1, 5):
        out += COEF[r] * (np.eye(n, k=r) + np.eye(n, k=-r))
    return out


def squares_of(n):
    m = (np.arange(n) + 1) // 2
    return (m * (2.0 * math.pi / (n * SPACING))) ** 2


def dot(a, b):
    return jnp.dot(a, b, precision=HIGHEST, preferred_element_type=jnp.float32)


def wrap(value, n):
    return jnp.where(value >= n, value - n, value)


def layout(nx, ny, nz):
    rows, places = 0, {}
    for name, count in (
        ("wy0", ny),
        ("wy1", ny),
        ("iy0", ny),
        ("iy1", ny),
        ("rz", nz),
        ("rzt", nz),
        ("rx", nx),
        ("rxt", nx),
        ("qx", nx),
        ("qz", 8),
    ):
        places[name] = (rows, count)
        rows += -(-count // 8) * 8
    return places, rows


def kernel(
    dims,
    occ_ref,
    orb_ref,
    pot_hbm,
    dz_hbm,
    dy_hbm,
    table_hbm,
    new_ref,
    out_ref,
    buf,
    res,
    pot_ref,
    dz_ref,
    dy_ref,
    tab,
    m1,
    r1,
    s1,
    r2,
    s2,
    r3,
    xs,
    y3,
    r4,
    m5,
    r5,
    s5,
    r6,
    load,
    store,
    token,
    send0,
    recv0,
    send1,
    recv1,
    send2,
    recv2,
    send3,
    recv3,
    send4,
    recv4,
    send5,
    recv5,
    send6,
    recv6,
):
    A, B, C, D, planes, ny, nz = dims
    nx = planes * D
    half = planes // 2
    groups = B * C
    keep = ny // groups
    rows_a = ny // A
    rows_own = ny // (A * groups)
    line = A * D
    stride = line // keep
    last = 4 + planes
    places, _ = layout(nx, ny, nz)

    orb = lax.axis_index("orb")
    dom = lax.axis_index("dom")
    a = orb // groups
    b = lax.rem(orb // C, B)
    c = lax.rem(orb, C)
    inner = orb - a * groups
    me = a * D + dom
    odd = lax.rem(dom, 2)
    fast_id = dom + 1 - 2 * odd
    slow_id = dom - 1 + 2 * odd
    has_slow = jnp.logical_and(slow_id >= 0, slow_id < D)
    base_fast = (1 - odd) * (planes - 4)
    base_slow = odd * (planes - 4)
    size = (B, C)
    mine = (b, c)

    def along(axis, offset):
        if axis == 0:
            return {"orb": a * groups + wrap(b + offset, B) * C + c}
        return {"orb": a * groups + b * C + wrap(c + offset, C)}

    def on_line(offset):
        slab = dom + offset % D
        over = (slab >= D).astype(jnp.int32)
        slab = slab - D * over
        block = wrap(a + offset // D + over, A)
        return {"orb": block * groups + inner, "dom": slab}, block * D + slab, slab

    barrier = pltpu.get_barrier_semaphore()
    for offset in (1, line - 1):
        pl.semaphore_signal(barrier, inc=1, device_id=on_line(offset)[0], device_id_type=MESH)
    for axis in range(2):
        for o in range(1, size[axis]):
            pl.semaphore_signal(barrier, inc=1, device_id=along(axis, o), device_id_type=MESH)
    loads = [
        pltpu.make_async_copy(orb_ref.at[0, 0], buf.at[0, 0, pl.ds(4, planes)], load.at[0]),
        pltpu.make_async_copy(orb_ref.at[0, 1], buf.at[0, 1, pl.ds(4, planes)], load.at[1]),
        pltpu.make_async_copy(dz_hbm, dz_ref, load.at[2]),
        pltpu.make_async_copy(dy_hbm, dy_ref, load.at[3]),
        pltpu.make_async_copy(pot_hbm, pot_ref, load.at[4]),
        pltpu.make_async_copy(table_hbm, tab, load.at[5]),
    ]
    for copy in loads:
        copy.start()
    pl.semaphore_wait(barrier, B + C)

    def halo(k, ch, side):
        base = base_slow if side else base_fast
        dst = jnp.where(odd == (0 if side else 1), last, 0)
        if k == 0:
            src = orb_ref.at[0, ch, pl.ds(base, 4)]
        else:
            src = buf.at[k, ch, pl.ds(4 + base, 4)]
        return pltpu.make_async_remote_copy(
            src_ref=src,
            dst_ref=buf.at[k, ch, pl.ds(dst, 4)],
            send_sem=send0.at[k, ch, side],
            recv_sem=recv0.at[k, ch, side],
            device_id={"dom": slow_id if side else fast_id},
            device_id_type=MESH,
        )

    def guarded(side, act):
        if side:
            pl.when(has_slow)(act)
        else:
            act()

    def start(k, ch, side):
        guarded(side, lambda: halo(k, ch, side).start())

    def arrived(k, ch, side):
        guarded(side, lambda: halo(k, ch, side).wait_recv())

    for ch in range(2):
        start(0, ch, 1)
    for ch in range(2):
        start(0, ch, 0)

    def tell(r):
        reach = 2**r
        for offset in (reach, line - reach):
            pl.semaphore_signal(token.at[r], inc=1, device_id=on_line(offset)[0], device_id_type=MESH)

    def told(r):
        pl.semaphore_wait(token.at[r], 2)

    rounds = max(1, (line // 2).bit_length() - 1)
    tell(0)

    @pl.when(jnp.logical_not(has_slow))
    def _():
        edge = odd * last
        for k in range(3):
            for ch in range(2):
                buf[k, ch, pl.ds(edge, 4)] = jnp.zeros((4, ny, nz), jnp.float32)

    def step(k, ch, x):
        f = buf[k, ch, 4 + x]
        high = f.astype(jnp.bfloat16)
        low = (f - high.astype(jnp.float32)).astype(jnp.bfloat16)
        h = jnp.dot(jnp.concatenate([high, low], axis=1), dz_ref[...], preferred_element_type=jnp.float32)
        h = h + jnp.dot(dy_ref[...], jnp.concatenate([high, low], axis=0), preferred_element_type=jnp.float32)
        h = h + (3.0 * COEF[0] + pot_ref[x]) * f
        for r in range(1, 5):
            h = h + COEF[r] * (buf[k, ch, 4 + x + r] + buf[k, ch, 4 + x - r])
        sign = 1.0 if (k + ch) % 2 else -1.0
        return (sign * TIME_STEP / (k + 1)) * h

    weight = occ_ref[0] * (1.0 / math.sqrt(A * groups))

    def sweep(k, ch, base):
        def body(i, carry):
            x = base + i
            out = step(k, ch, x)
            if k < 2:
                buf[k + 1, ch, 4 + x] = out
            elif ch == 0:
                res[1, x] = ((buf[0, 1, 4 + x] + buf[1, 0, 4 + x]) + buf[2, 1, 4 + x]) + out
            else:
                real = ((buf[0, 0, 4 + x] + buf[1, 1, 4 + x]) + buf[2, 0, 4 + x]) + out
                res[0, x] = real
                imag = res[1, x]
                m1[i // 2, base // 2 + lax.rem(i, 2)] = weight * (real * real + imag * imag)
            return carry

        lax.fori_loop(0, 4, body, 0, unroll=4)
        if k == 2 and ch == 1:
            for h in range(2):
                first, count = places["wy%d" % h]
                for i in range(2):
                    at = base // 2 + i
                    m1[h, at] = dot(tab[first : first + count, :ny], m1[h, at])

    def middle(k, ch):
        for base in range(4, planes - 4, 4):
            sweep(k, ch, base)

    def edge_of(k, ch, side):
        arrived(k, ch, side)
        sweep(k, ch, base_slow if side else base_fast)
        if k < 2:
            start(k + 1, ch, side)

    loads[2].wait()
    loads[3].wait()
    loads[4].wait()
    for ch in range(2):
        loads[ch].wait()
        middle(0, ch)
    for ch in range(2):
        edge_of(0, ch, 0)
    told(0)
    if rounds > 1:
        tell(1)
    edge_of(0, 0, 1)
    middle(1, 0)
    edge_of(1, 0, 0)
    edge_of(0, 1, 1)
    middle(1, 1)
    edge_of(1, 1, 0)
    if rounds > 1:
        told(1)
    if rounds > 2:
        tell(2)
    edge_of(1, 0, 1)
    edge_of(1, 1, 1)
    if rounds > 2:
        told(2)
    if rounds > 3:
        tell(3)
    loads[5].wait()
    for ch in range(2):
        middle(2, ch)
        edge_of(2, ch, 0)

    early = planes // 2 - 2
    starts = ((1 - odd) * 2, odd * early)
    counts = (early, 2)

    def first_hop(t, h, o):
        axis = h
        big = ny // size[axis]
        peer = wrap(mine[axis] + o, size[axis])
        part = pl.ds(starts[t], counts[t])
        return pltpu.make_async_remote_copy(
            src_ref=m1.at[h, part, pl.ds(pl.multiple_of(peer * big, 8), big)],
            dst_ref=r1.at[h, o - 1, part],
            send_sem=send1.at[t, h, o - 1],
            recv_sem=recv1.at[t, h, o - 1],
            device_id=along(axis, o),
            device_id_type=MESH,
        )

    def second_hop(t, h, o):
        axis = 1 - h
        peer = wrap(mine[axis] + o, size[axis])
        part = pl.ds(starts[t], counts[t])
        return pltpu.make_async_remote_copy(
            src_ref=s1.at[h, part, pl.ds(pl.multiple_of(peer * keep, 8), keep)],
            dst_ref=r2.at[h, o - 1, part],
            send_sem=send2.at[t, h, o - 1],
            recv_sem=recv2.at[t, h, o - 1],
            device_id=along(axis, o),
            device_id_type=MESH,
        )

    def offsets(n):
        return sorted(range(1, n), key=lambda o: -min(o, n - o))

    def each(t, make, act):
        for h in range(2):
            axis = h if make in (first_hop, third_hop) else 1 - h
            for o in offsets(size[axis]):
                act(make(t, h, o))

    def begin(copy):
        copy.start()

    def left(copy):
        copy.wait_send()

    def third_hop(t, h, o):
        axis = h
        big = rows_a // size[axis]
        peer = wrap(mine[axis] + o, size[axis])
        return pltpu.make_async_remote_copy(
            src_ref=m5.at[h, :, pl.ds(pl.multiple_of(a * rows_a + peer * big, 8), big)],
            dst_ref=r5.at[h, o - 1],
            send_sem=send5.at[h, o - 1],
            recv_sem=recv5.at[h, o - 1],
            device_id=along(axis, o),
            device_id_type=MESH,
        )

    def fourth_hop(t, h, o):
        axis = 1 - h
        peer = wrap(mine[axis] + o, size[axis])
        return pltpu.make_async_remote_copy(
            src_ref=s5.at[h, peer],
            dst_ref=r6.at[h, o - 1],
            send_sem=send6.at[h, o - 1],
            recv_sem=recv6.at[h, o - 1],
            device_id=along(axis, o),
            device_id_type=MESH,
        )

    each(0, first_hop, begin)
    edge_of(2, 0, 1)
    pltpu.make_async_copy(res.at[1], new_ref.at[0, 1], store.at[1]).start()
    edge_of(2, 1, 1)
    each(1, first_hop, begin)
    pltpu.make_async_copy(res.at[0], new_ref.at[0, 0], store.at[0]).start()
    for t in range(2):
        part = pl.ds(starts[t], counts[t])
        for h in range(2):
            axis = h
            big = ny // size[axis]
            total = m1[h, part, pl.ds(pl.multiple_of(mine[axis] * big, 8), big)]
            for o in range(1, size[axis]):
                first_hop(t, h, o).wait_recv()
                total = total + r1[h, o - 1, part]
            s1[h, part] = total
            for o in offsets(size[1 - h]):
                second_hop(t, h, o).start()
    each(0, second_hop, lambda copy: copy.wait_recv())
    each(1, second_hop, lambda copy: copy.wait_recv())
    for h in range(2):
        axis = 1 - h
        total = s1[h, :, pl.ds(pl.multiple_of(mine[axis] * keep, 8), keep)]
        for o in range(1, size[axis]):
            total = total + r2[h, o - 1]
        for p in range(half):
            s2[:, (p // 2) * 4 + 2 * h + p % 2, :] = total[p]

    if rounds > 3:
        told(3)
    own = me // stride
    solver = lax.rem(me, stride) == 0

    def to_solver(i):
        j = wrap(own + i, keep)
        place = j * stride
        block = place // D
        return pltpu.make_async_remote_copy(
            src_ref=s2.at[j],
            dst_ref=r3.at[me],
            send_sem=send3.at[i],
            recv_sem=recv3.at[me],
            device_id={"orb": block * groups + inner, "dom": place - block * D},
            device_id_type=MESH,
        )

    for i in sorted(range(1, keep), key=lambda i: -min(i, keep - i)):
        to_solver(i).start()

    @pl.when(jnp.logical_not(solver))
    def _():
        to_solver(0).start()

    def to_slab(offset):
        device, place, slab = on_line(offset)
        return pltpu.make_async_remote_copy(
            src_ref=y3.at[slab],
            dst_ref=r4.at[own],
            send_sem=send4.at[offset],
            recv_sem=recv4.at[own],
            device_id=device,
            device_id_type=MESH,
        )

    far_first = sorted(range(1, line), key=lambda o: -min(o // 2, line // 2 - o // 2))

    @pl.when(solver)
    def _():
        r3[me] = s2[own]
        for offset in range(1, line):
            device, place, slab = on_line(offset)
            pltpu.make_async_remote_copy(
                src_ref=s2.at[0],
                dst_ref=r3.at[place],
                send_sem=send3.at[0],
                recv_sem=recv3.at[place],
                device_id=device,
                device_id_type=MESH,
            ).wait_recv()
        for slab in range(D):
            piece = r3[slab]
            for q in range(1, A):
                piece = piece + r3[q * D + slab]
            xs[slab * planes : (slab + 1) * planes, :] = piece

        def table(name):
            first, count = places[name]
            return tab[first : first + count, :]

        modes = dot(table("rx")[:, :nx], dot(xs[...], table("rzt")))
        wave = inner * keep + own
        m = ((wave + 1) // 2).astype(jnp.float32) * (2.0 * math.pi / (ny * SPACING))
        squares = (table("qx") + m * m) + table("qz")[:1]
        positive = squares > 0.0
        solved = modes * jnp.where(positive, 4.0 * math.pi / jnp.where(positive, squares, 1.0), 0.0)
        xs[...] = dot(dot(table("rxt")[:, :nx], solved), table("rz"))
        for slab in range(D):
            y3[slab] = xs[slab * planes : (slab + 1) * planes, :]
        for offset in far_first:
            to_slab(offset).start()
        r4[own] = y3[dom]

    def from_solver(i):
        j = wrap(own + i, keep)
        place = j * stride
        block = place // D
        return pltpu.make_async_remote_copy(
            src_ref=y3.at[0],
            dst_ref=r4.at[j],
            send_sem=send4.at[0],
            recv_sem=recv4.at[j],
            device_id={"orb": block * groups + inner, "dom": place - block * D},
            device_id_type=MESH,
        )

    for i in range(1, keep):
        from_solver(i).wait_recv()

    @pl.when(jnp.logical_not(solver))
    def _():
        from_solver(0).wait_recv()

    for h in range(2):
        table = tab[pl.ds(pl.multiple_of(places["iy%d" % h][0] + inner * keep, 8), keep), :]
        for p in range(half):
            rows = r4[:, (p // 2) * 4 + 2 * h + p % 2, :]
            m5[h, p] = lax.dot_general(
                table, rows, (((0,), (0,)), ((), ())), precision=HIGHEST, preferred_element_type=jnp.float32
            )[:ny]
        for o in offsets(size[h]):
            third_hop(0, h, o).start()
    for h in range(2):
        axis = h
        big = rows_a // size[axis]
        total = m5[h, :, pl.ds(pl.multiple_of(a * rows_a + mine[axis] * big, 8), big)]
        for o in range(1, size[axis]):
            third_hop(0, h, o).wait_recv()
            total = total + r5[h, o - 1]
        for p in range(size[1 - h]):
            s5[h, p] = total[:, p * rows_own : (p + 1) * rows_own]
        for o in offsets(size[1 - h]):
            fourth_hop(0, h, o).start()
    for h in range(2):
        axis = 1 - h
        total = s5[h, mine[axis]]
        for o in range(1, size[axis]):
            fourth_hop(0, h, o).wait_recv()
            total = total + r6[h, o - 1]
        for p in range(half):
            out_ref[(p // 2) * 4 + 2 * h + p % 2] = total[p]

    for k in range(3):
        for ch in range(2):
            for side in range(2):
                guarded(side, lambda k=k, ch=ch, side=side: halo(k, ch, side).wait_send())
    for t in range(2):
        each(t, first_hop, left)
        each(t, second_hop, left)
    each(0, third_hop, left)
    each(0, fourth_hop, left)
    for i in range(1, keep):
        to_solver(i).wait_send()

    @pl.when(jnp.logical_not(solver))
    def _():
        to_solver(0).wait_send()

    @pl.when(solver)
    def _():
        for offset in far_first:
            to_slab(offset).wait_send()

    for part in range(2):
        pltpu.make_async_copy(res.at[part], new_ref.at[0, part], store.at[part]).wait()


def factors(orbs):
    return {64: (4, 4, 4), 8: (2, 2, 2)}[orbs]


def body(orbitals, occupations, potential):
    groups = lax.axis_size("orb")
    doms = lax.axis_size("dom")
    A, B, C = factors(groups)
    planes, ny, nz = potential.shape
    nx = planes * doms
    half = planes // 2
    keep = ny // (B * C)
    rows_own = ny // groups
    line = A * doms
    f32 = jnp.float32
    vmem = pl.BlockSpec(memory_space=pltpu.VMEM)
    hbm = pl.BlockSpec(memory_space=pltpu.HBM)
    dma = pltpu.SemaphoreType.DMA

    dz = band(nz)
    dy = band(ny)
    ry = real_basis(ny)
    rz = real_basis(nz)
    rx = real_basis(nx)
    swapped = ry.reshape(B, C, keep, ny).transpose(1, 0, 2, 3).reshape(ny, ny)
    back = ry.reshape(ny, A, B, C, rows_own).transpose(0, 1, 3, 2, 4).reshape(ny, ny)
    places, rows = layout(nx, ny, nz)
    table = np.zeros((rows, max(ny, nz, nx)), np.float32)
    for name, value in (
        ("wy0", ry),
        ("wy1", swapped),
        ("iy0", ry),
        ("iy1", back),
        ("rz", rz),
        ("rzt", rz.T),
        ("rx", rx),
        ("rxt", rx.T),
        ("qx", squares_of(nx)[:, None] * np.ones((1, nz))),
        ("qz", squares_of(nz)[None, :]),
    ):
        first = places[name][0]
        table[first : first + value.shape[0], : value.shape[1]] = value
    scratch = [
        pltpu.VMEM((3, 2, planes + 8, ny, nz), f32),
        pltpu.VMEM((2, planes, ny, nz), f32),
        pltpu.VMEM((planes, ny, nz), f32),
        pltpu.VMEM((2 * nz, nz), jnp.bfloat16),
        pltpu.VMEM((ny, 2 * ny), jnp.bfloat16),
        pltpu.VMEM(table.shape, f32),
        pltpu.VMEM((2, half, ny, nz), f32),
        pltpu.VMEM((2, B - 1, half, ny // B, nz), f32),
        pltpu.VMEM((2, half, ny // B, nz), f32),
        pltpu.VMEM((2, B - 1, half, keep, nz), f32),
        pltpu.VMEM((keep, planes, nz), f32),
        pltpu.VMEM((line, planes, nz), f32),
        pltpu.VMEM((nx, nz), f32),
        pltpu.VMEM((doms, planes, nz), f32),
        pltpu.VMEM((keep, planes, nz), f32),
        pltpu.VMEM((2, half, ny, nz), f32),
        pltpu.VMEM((2, B - 1, half, ny // (A * B), nz), f32),
        pltpu.VMEM((2, B, half, rows_own, nz), f32),
        pltpu.VMEM((2, B - 1, half, rows_own, nz), f32),
        dma((6,)),
        dma((2,)),
        pltpu.SemaphoreType.REGULAR((4,)),
        dma((3, 2, 2)),
        dma((3, 2, 2)),
        dma((2, 2, B - 1)),
        dma((2, 2, B - 1)),
        dma((2, 2, B - 1)),
        dma((2, 2, B - 1)),
        dma((keep,)),
        dma((line,)),
        dma((line,)),
        dma((keep,)),
        dma((2, B - 1)),
        dma((2, B - 1)),
        dma((2, B - 1)),
        dma((2, B - 1)),
    ]
    return pl.pallas_call(
        functools.partial(kernel, (A, B, C, doms, planes, ny, nz)),
        out_shape=(
            jax.ShapeDtypeStruct(orbitals.shape, f32),
            jax.ShapeDtypeStruct((planes, rows_own, nz), f32),
        ),
        in_specs=[pl.BlockSpec(memory_space=pltpu.SMEM)] + [hbm] * 5,
        out_specs=(hbm, vmem),
        scratch_shapes=scratch,
        compiler_params=pltpu.CompilerParams(
            collective_id=0, has_side_effects=True, vmem_limit_bytes=60 * 2**20
        ),
    )(
        occupations,
        orbitals,
        potential,
        jnp.asarray(np.concatenate([dz, dz], axis=0), jnp.bfloat16),
        jnp.asarray(np.concatenate([dy, dy], axis=1), jnp.bfloat16),
        jnp.asarray(table),
    )


def solution(mesh):
    return jax.shard_map(
        body,
        mesh=mesh,
        in_specs=(P("orb", None, "dom", None, None), P("orb"), P("dom", None, None)),
        out_specs=(P("orb", None, "dom", None, None), P("dom", "orb", None)),
        check_vma=False,
    )
```

```python
import functools
import math

import jax
import jax.numpy as jnp
import numpy as np
from jax import lax
from jax.experimental import pallas as pl
from jax.experimental.pallas import tpu as pltpu
from jax.sharding import PartitionSpec as P

MESH = pl.DeviceIdType.MESH
HIGHEST = lax.Precision.HIGHEST
SPACING = 0.4
TIME_STEP = 0.03
STENCIL = (-205.0 / 72.0, 8.0 / 5.0, -1.0 / 5.0, 8.0 / 315.0, -1.0 / 560.0)
COEF = tuple(-0.5 * c / (SPACING * SPACING) for c in STENCIL)


def real_basis(n):
    grid = np.arange(n)
    rows = np.zeros((n, n))
    for k in range(n):
        m = (k + 1) // 2
        angle = 2.0 * np.pi * ((m * grid) % n) / n
        wave = np.cos(angle) if (k % 2 == 1 or k == 0) else np.sin(angle)
        rows[k] = wave * (np.sqrt(1.0 / n) if m in (0, n // 2) else np.sqrt(2.0 / n))
    return rows


def band(n):
    out = np.zeros((n, n))
    for r in range(1, 5):
        out += COEF[r] * (np.eye(n, k=r) + np.eye(n, k=-r))
    return out


def squares_of(n):
    m = (np.arange(n) + 1) // 2
    return (m * (2.0 * math.pi / (n * SPACING))) ** 2


def dot(a, b):
    return jnp.dot(a, b, precision=HIGHEST, preferred_element_type=jnp.float32)


def wrap(value, n):
    return jnp.where(value >= n, value - n, value)


def layout(nx, ny, nz):
    rows, places = 0, {}
    for name, count in (
        ("wy0", ny),
        ("wy1", ny),
        ("iy0", ny),
        ("iy1", ny),
        ("rz", nz),
        ("rzt", nz),
        ("rx", nx),
        ("rxt", nx),
        ("qx", nx),
        ("qz", 8),
    ):
        places[name] = (rows, count)
        rows += -(-count // 8) * 8
    return places, rows


def kernel(
    dims,
    occ_ref,
    orb_ref,
    pot_hbm,
    dz_hbm,
    dy_hbm,
    table_hbm,
    new_ref,
    out_ref,
    buf,
    res,
    pot_ref,
    dz_ref,
    dy_ref,
    tab,
    m1,
    r1,
    s1,
    r2,
    s2,
    r3,
    xs,
    y3,
    r4,
    m5,
    r5,
    s5,
    r6,
    load,
    store,
    token,
    send0,
    recv0,
    send1,
    recv1,
    send2,
    recv2,
    send3,
    recv3,
    send4,
    recv4,
    send5,
    recv5,
    send6,
    recv6,
):
    A, B, C, D, planes, ny, nz = dims
    nx = planes * D
    half = planes // 2
    groups = B * C
    keep = ny // groups
    rows_a = ny // A
    rows_own = ny // (A * groups)
    line = A * D
    stride = line // keep
    last = 4 + planes
    places, _ = layout(nx, ny, nz)

    orb = lax.axis_index("orb")
    dom = lax.axis_index("dom")
    a = orb // groups
    b = lax.rem(orb // C, B)
    c = lax.rem(orb, C)
    inner = orb - a * groups
    me = a * D + dom
    odd = lax.rem(dom, 2)
    fast_id = dom + 1 - 2 * odd
    slow_id = dom - 1 + 2 * odd
    has_slow = jnp.logical_and(slow_id >= 0, slow_id < D)
    base_fast = (1 - odd) * (planes - 4)
    base_slow = odd * (planes - 4)
    size = (B, C)
    mine = (b, c)

    def along(axis, offset):
        if axis == 0:
            return {"orb": a * groups + wrap(b + offset, B) * C + c}
        return {"orb": a * groups + b * C + wrap(c + offset, C)}

    def on_line(offset):
        slab = dom + offset % D
        over = (slab >= D).astype(jnp.int32)
        slab = slab - D * over
        block = wrap(a + offset // D + over, A)
        return {"orb": block * groups + inner, "dom": slab}, block * D + slab, slab

    barrier = pltpu.get_barrier_semaphore()
    for offset in (1, line - 1):
        pl.semaphore_signal(barrier, inc=1, device_id=on_line(offset)[0], device_id_type=MESH)
    for axis in range(2):
        for o in range(1, size[axis]):
            pl.semaphore_signal(barrier, inc=1, device_id=along(axis, o), device_id_type=MESH)
    loads = [
        pltpu.make_async_copy(orb_ref.at[0, 0], buf.at[0, 0, pl.ds(4, planes)], load.at[0]),
        pltpu.make_async_copy(orb_ref.at[0, 1], buf.at[0, 1, pl.ds(4, planes)], load.at[1]),
        pltpu.make_async_copy(dz_hbm, dz_ref, load.at[2]),
        pltpu.make_async_copy(dy_hbm, dy_ref, load.at[3]),
        pltpu.make_async_copy(pot_hbm, pot_ref, load.at[4]),
        pltpu.make_async_copy(table_hbm, tab, load.at[5]),
    ]
    for copy in loads:
        copy.start()
    pl.semaphore_wait(barrier, B + C)

    def halo(k, ch, side):
        base = base_slow if side else base_fast
        dst = jnp.where(odd == (0 if side else 1), last, 0)
        if k == 0:
            src = orb_ref.at[0, ch, pl.ds(base, 4)]
        else:
            src = buf.at[k, ch, pl.ds(4 + base, 4)]
        return pltpu.make_async_remote_copy(
            src_ref=src,
            dst_ref=buf.at[k, ch, pl.ds(dst, 4)],
            send_sem=send0.at[k, ch, side],
            recv_sem=recv0.at[k, ch, side],
            device_id={"dom": slow_id if side else fast_id},
            device_id_type=MESH,
        )

    def guarded(side, act):
        if side:
            pl.when(has_slow)(act)
        else:
            act()

    def start(k, ch, side):
        guarded(side, lambda: halo(k, ch, side).start())

    def arrived(k, ch, side):
        guarded(side, lambda: halo(k, ch, side).wait_recv())

    for ch in range(2):
        start(0, ch, 1)
    for ch in range(2):
        start(0, ch, 0)

    def tell(r):
        reach = 2**r
        for offset in (reach, line - reach):
            pl.semaphore_signal(token.at[r], inc=1, device_id=on_line(offset)[0], device_id_type=MESH)

    def told(r):
        pl.semaphore_wait(token.at[r], 2)

    rounds = max(1, (line // 2).bit_length() - 1)
    tell(0)

    @pl.when(jnp.logical_not(has_slow))
    def _():
        edge = odd * last
        for k in range(3):
            for ch in range(2):
                buf[k, ch, pl.ds(edge, 4)] = jnp.zeros((4, ny, nz), jnp.float32)

    def step(k, ch, x):
        f = buf[k, ch, 4 + x]
        high = f.astype(jnp.bfloat16)
        low = (f - high.astype(jnp.float32)).astype(jnp.bfloat16)
        h = jnp.dot(jnp.concatenate([high, low], axis=1), dz_ref[...], preferred_element_type=jnp.float32)
        h = h + jnp.dot(dy_ref[...], jnp.concatenate([high, low], axis=0), preferred_element_type=jnp.float32)
        h = h + (3.0 * COEF[0] + pot_ref[x]) * f
        for r in range(1, 5):
            h = h + COEF[r] * (buf[k, ch, 4 + x + r] + buf[k, ch, 4 + x - r])
        sign = 1.0 if (k + ch) % 2 else -1.0
        return (sign * TIME_STEP / (k + 1)) * h

    weight = occ_ref[0] * (1.0 / math.sqrt(A * groups))

    def sweep(k, ch, base):
        def body(i, carry):
            x = base + i
            out = step(k, ch, x)
            if k < 2:
                buf[k + 1, ch, 4 + x] = out
            elif ch == 0:
                res[1, x] = ((buf[0, 1, 4 + x] + buf[1, 0, 4 + x]) + buf[2, 1, 4 + x]) + out
            else:
                real = ((buf[0, 0, 4 + x] + buf[1, 1, 4 + x]) + buf[2, 0, 4 + x]) + out
                res[0, x] = real
                imag = res[1, x]
                m1[i // 2, base // 2 + lax.rem(i, 2)] = weight * (real * real + imag * imag)
            return carry

        lax.fori_loop(0, 4, body, 0, unroll=4)
        if k == 2 and ch == 1:
            for h in range(2):
                first, count = places["wy%d" % h]
                for i in range(2):
                    at = base // 2 + i
                    m1[h, at] = dot(tab[first : first + count, :ny], m1[h, at])

    def middle(k, ch):
        for base in range(4, planes - 4, 4):
            sweep(k, ch, base)

    def edge_of(k, ch, side):
        arrived(k, ch, side)
        sweep(k, ch, base_slow if side else base_fast)
        if k < 2:
            start(k + 1, ch, side)

    loads[2].wait()
    loads[3].wait()
    loads[4].wait()
    for ch in range(2):
        loads[ch].wait()
        middle(0, ch)
    for ch in range(2):
        edge_of(0, ch, 0)
    told(0)
    if rounds > 1:
        tell(1)
    edge_of(0, 0, 1)
    middle(1, 0)
    edge_of(1, 0, 0)
    edge_of(0, 1, 1)
    middle(1, 1)
    edge_of(1, 1, 0)
    if rounds > 1:
        told(1)
    if rounds > 2:
        tell(2)
    edge_of(1, 0, 1)
    middle(2, 0)
    edge_of(2, 0, 0)
    edge_of(1, 1, 1)
    loads[5].wait()
    middle(2, 1)
    edge_of(2, 1, 0)

    early = planes // 2 - 2
    starts = ((1 - odd) * 2, odd * early)
    counts = (early, 2)

    def first_hop(t, h, o):
        axis = h
        big = ny // size[axis]
        peer = wrap(mine[axis] + o, size[axis])
        part = pl.ds(starts[t], counts[t])
        return pltpu.make_async_remote_copy(
            src_ref=m1.at[h, part, pl.ds(pl.multiple_of(peer * big, 8), big)],
            dst_ref=r1.at[h, o - 1, part],
            send_sem=send1.at[t, h, o - 1],
            recv_sem=recv1.at[t, h, o - 1],
            device_id=along(axis, o),
            device_id_type=MESH,
        )

    def second_hop(t, h, o):
        axis = 1 - h
        peer = wrap(mine[axis] + o, size[axis])
        part = pl.ds(starts[t], counts[t])
        return pltpu.make_async_remote_copy(
            src_ref=s1.at[h, part, pl.ds(pl.multiple_of(peer * keep, 8), keep)],
            dst_ref=r2.at[h, o - 1, part],
            send_sem=send2.at[t, h, o - 1],
            recv_sem=recv2.at[t, h, o - 1],
            device_id=along(axis, o),
            device_id_type=MESH,
        )

    def offsets(n):
        return sorted(range(1, n), key=lambda o: -min(o, n - o))

    def each(t, make, act):
        for h in range(2):
            axis = h if make in (first_hop, third_hop) else 1 - h
            for o in offsets(size[axis]):
                act(make(t, h, o))

    def begin(copy):
        copy.start()

    def left(copy):
        copy.wait_send()

    def third_hop(t, h, o):
        axis = h
        big = rows_a // size[axis]
        peer = wrap(mine[axis] + o, size[axis])
        return pltpu.make_async_remote_copy(
            src_ref=m5.at[h, :, pl.ds(pl.multiple_of(a * rows_a + peer * big, 8), big)],
            dst_ref=r5.at[h, o - 1],
            send_sem=send5.at[h, o - 1],
            recv_sem=recv5.at[h, o - 1],
            device_id=along(axis, o),
            device_id_type=MESH,
        )

    def fourth_hop(t, h, o):
        axis = 1 - h
        peer = wrap(mine[axis] + o, size[axis])
        return pltpu.make_async_remote_copy(
            src_ref=s5.at[h, peer],
            dst_ref=r6.at[h, o - 1],
            send_sem=send6.at[h, o - 1],
            recv_sem=recv6.at[h, o - 1],
            device_id=along(axis, o),
            device_id_type=MESH,
        )

    each(0, first_hop, begin)
    if rounds > 2:
        told(2)
    if rounds > 3:
        tell(3)
    edge_of(2, 0, 1)
    pltpu.make_async_copy(res.at[1], new_ref.at[0, 1], store.at[1]).start()
    edge_of(2, 1, 1)
    each(1, first_hop, begin)
    pltpu.make_async_copy(res.at[0], new_ref.at[0, 0], store.at[0]).start()
    for t in range(2):
        part = pl.ds(starts[t], counts[t])
        for h in range(2):
            axis = h
            big = ny // size[axis]
            total = m1[h, part, pl.ds(pl.multiple_of(mine[axis] * big, 8), big)]
            for o in range(1, size[axis]):
                first_hop(t, h, o).wait_recv()
                total = total + r1[h, o - 1, part]
            s1[h, part] = total
            for o in offsets(size[1 - h]):
                second_hop(t, h, o).start()
    each(0, second_hop, lambda copy: copy.wait_recv())
    each(1, second_hop, lambda copy: copy.wait_recv())
    for h in range(2):
        axis = 1 - h
        total = s1[h, :, pl.ds(pl.multiple_of(mine[axis] * keep, 8), keep)]
        for o in range(1, size[axis]):
            total = total + r2[h, o - 1]
        for p in range(half):
            s2[:, (p // 2) * 4 + 2 * h + p % 2, :] = total[p]

    if rounds > 3:
        told(3)
    own = me // stride
    solver = lax.rem(me, stride) == 0

    def to_solver(i):
        j = wrap(own + i, keep)
        place = j * stride
        block = place // D
        return pltpu.make_async_remote_copy(
            src_ref=s2.at[j],
            dst_ref=r3.at[me],
            send_sem=send3.at[i],
            recv_sem=recv3.at[me],
            device_id={"orb": block * groups + inner, "dom": place - block * D},
            device_id_type=MESH,
        )

    for i in sorted(range(1, keep), key=lambda i: -min(i, keep - i)):
        to_solver(i).start()

    @pl.when(jnp.logical_not(solver))
    def _():
        to_solver(0).start()

    def to_slab(offset):
        device, place, slab = on_line(offset)
        return pltpu.make_async_remote_copy(
            src_ref=y3.at[slab],
            dst_ref=r4.at[own],
            send_sem=send4.at[offset],
            recv_sem=recv4.at[own],
            device_id=device,
            device_id_type=MESH,
        )

    far_first = sorted(range(1, line), key=lambda o: -min(o // 2, line // 2 - o // 2))

    @pl.when(solver)
    def _():
        r3[me] = s2[own]
        for offset in range(1, line):
            device, place, slab = on_line(offset)
            pltpu.make_async_remote_copy(
                src_ref=s2.at[0],
                dst_ref=r3.at[place],
                send_sem=send3.at[0],
                recv_sem=recv3.at[place],
                device_id=device,
                device_id_type=MESH,
            ).wait_recv()
        for slab in range(D):
            piece = r3[slab]
            for q in range(1, A):
                piece = piece + r3[q * D + slab]
            xs[slab * planes : (slab + 1) * planes, :] = piece

        def table(name):
            first, count = places[name]
            return tab[first : first + count, :]

        modes = dot(table("rx")[:, :nx], dot(xs[...], table("rzt")))
        wave = inner * keep + own
        m = ((wave + 1) // 2).astype(jnp.float32) * (2.0 * math.pi / (ny * SPACING))
        squares = (table("qx") + m * m) + table("qz")[:1]
        positive = squares > 0.0
        solved = modes * jnp.where(positive, 4.0 * math.pi / jnp.where(positive, squares, 1.0), 0.0)
        xs[...] = dot(dot(table("rxt")[:, :nx], solved), table("rz"))
        for slab in range(D):
            y3[slab] = xs[slab * planes : (slab + 1) * planes, :]
        for offset in far_first:
            to_slab(offset).start()
        r4[own] = y3[dom]

    def from_solver(i):
        j = wrap(own + i, keep)
        place = j * stride
        block = place // D
        return pltpu.make_async_remote_copy(
            src_ref=y3.at[0],
            dst_ref=r4.at[j],
            send_sem=send4.at[0],
            recv_sem=recv4.at[j],
            device_id={"orb": block * groups + inner, "dom": place - block * D},
            device_id_type=MESH,
        )

    for i in range(1, keep):
        from_solver(i).wait_recv()

    @pl.when(jnp.logical_not(solver))
    def _():
        from_solver(0).wait_recv()

    for h in range(2):
        table = tab[pl.ds(pl.multiple_of(places["iy%d" % h][0] + inner * keep, 8), keep), :]
        for p in range(half):
            rows = r4[:, (p // 2) * 4 + 2 * h + p % 2, :]
            m5[h, p] = lax.dot_general(
                table, rows, (((0,), (0,)), ((), ())), precision=HIGHEST, preferred_element_type=jnp.float32
            )[:ny]
        for o in offsets(size[h]):
            third_hop(0, h, o).start()
    for h in range(2):
        axis = h
        big = rows_a // size[axis]
        total = m5[h, :, pl.ds(pl.multiple_of(a * rows_a + mine[axis] * big, 8), big)]
        for o in range(1, size[axis]):
            third_hop(0, h, o).wait_recv()
            total = total + r5[h, o - 1]
        for p in range(size[1 - h]):
            s5[h, p] = total[:, p * rows_own : (p + 1) * rows_own]
        for o in offsets(size[1 - h]):
            fourth_hop(0, h, o).start()
    for h in range(2):
        axis = 1 - h
        total = s5[h, mine[axis]]
        for o in range(1, size[axis]):
            fourth_hop(0, h, o).wait_recv()
            total = total + r6[h, o - 1]
        for p in range(half):
            out_ref[(p // 2) * 4 + 2 * h + p % 2] = total[p]

    for k in range(3):
        for ch in range(2):
            for side in range(2):
                guarded(side, lambda k=k, ch=ch, side=side: halo(k, ch, side).wait_send())
    for t in range(2):
        each(t, first_hop, left)
        each(t, second_hop, left)
    each(0, third_hop, left)
    each(0, fourth_hop, left)
    for i in range(1, keep):
        to_solver(i).wait_send()

    @pl.when(jnp.logical_not(solver))
    def _():
        to_solver(0).wait_send()

    @pl.when(solver)
    def _():
        for offset in far_first:
            to_slab(offset).wait_send()

    for part in range(2):
        pltpu.make_async_copy(res.at[part], new_ref.at[0, part], store.at[part]).wait()


def finish_kernel(new_in, out_in, new_ref, out_ref, held, small, sems):
    cut = new_in.shape[2] // 4
    pieces = [(part, pl.ds(q * cut, cut)) for part in range(2) for q in range(4)]
    count = len(pieces)
    ins = [
        pltpu.make_async_copy(new_in.at[0, part, piece], held.at[part, piece], sems.at[0, i])
        for i, (part, piece) in enumerate(pieces)
    ]
    outs = [
        pltpu.make_async_copy(held.at[part, piece], new_ref.at[0, part, piece], sems.at[1, i])
        for i, (part, piece) in enumerate(pieces)
    ]
    ins.append(pltpu.make_async_copy(out_in, small, sems.at[0, count]))
    outs.append(pltpu.make_async_copy(small, out_ref, sems.at[1, count]))
    for copy in ins:
        copy.start()
    for first, second in zip(ins, outs):
        first.wait()
        second.start()
    for copy in outs:
        copy.wait()


def factors(orbs):
    return {64: (4, 4, 4), 8: (2, 2, 2)}[orbs]


def body(orbitals, occupations, potential):
    groups = lax.axis_size("orb")
    doms = lax.axis_size("dom")
    A, B, C = factors(groups)
    planes, ny, nz = potential.shape
    nx = planes * doms
    half = planes // 2
    keep = ny // (B * C)
    rows_own = ny // groups
    line = A * doms
    f32 = jnp.float32
    vmem = pl.BlockSpec(memory_space=pltpu.VMEM)
    hbm = pl.BlockSpec(memory_space=pltpu.HBM)
    dma = pltpu.SemaphoreType.DMA

    dz = band(nz)
    dy = band(ny)
    ry = real_basis(ny)
    rz = real_basis(nz)
    rx = real_basis(nx)
    swapped = ry.reshape(B, C, keep, ny).transpose(1, 0, 2, 3).reshape(ny, ny)
    back = ry.reshape(ny, A, B, C, rows_own).transpose(0, 1, 3, 2, 4).reshape(ny, ny)
    places, rows = layout(nx, ny, nz)
    table = np.zeros((rows, max(ny, nz, nx)), np.float32)
    for name, value in (
        ("wy0", ry),
        ("wy1", swapped),
        ("iy0", ry),
        ("iy1", back),
        ("rz", rz),
        ("rzt", rz.T),
        ("rx", rx),
        ("rxt", rx.T),
        ("qx", squares_of(nx)[:, None] * np.ones((1, nz))),
        ("qz", squares_of(nz)[None, :]),
    ):
        first = places[name][0]
        table[first : first + value.shape[0], : value.shape[1]] = value
    scratch = [
        pltpu.VMEM((3, 2, planes + 8, ny, nz), f32),
        pltpu.VMEM((2, planes, ny, nz), f32),
        pltpu.VMEM((planes, ny, nz), f32),
        pltpu.VMEM((2 * nz, nz), jnp.bfloat16),
        pltpu.VMEM((ny, 2 * ny), jnp.bfloat16),
        pltpu.VMEM(table.shape, f32),
        pltpu.VMEM((2, half, ny, nz), f32),
        pltpu.VMEM((2, B - 1, half, ny // B, nz), f32),
        pltpu.VMEM((2, half, ny // B, nz), f32),
        pltpu.VMEM((2, B - 1, half, keep, nz), f32),
        pltpu.VMEM((keep, planes, nz), f32),
        pltpu.VMEM((line, planes, nz), f32),
        pltpu.VMEM((nx, nz), f32),
        pltpu.VMEM((doms, planes, nz), f32),
        pltpu.VMEM((keep, planes, nz), f32),
        pltpu.VMEM((2, half, ny, nz), f32),
        pltpu.VMEM((2, B - 1, half, ny // (A * B), nz), f32),
        pltpu.VMEM((2, B, half, rows_own, nz), f32),
        pltpu.VMEM((2, B - 1, half, rows_own, nz), f32),
        dma((6,)),
        dma((2,)),
        pltpu.SemaphoreType.REGULAR((4,)),
        dma((3, 2, 2)),
        dma((3, 2, 2)),
        dma((2, 2, B - 1)),
        dma((2, 2, B - 1)),
        dma((2, 2, B - 1)),
        dma((2, 2, B - 1)),
        dma((keep,)),
        dma((line,)),
        dma((line,)),
        dma((keep,)),
        dma((2, B - 1)),
        dma((2, B - 1)),
        dma((2, B - 1)),
        dma((2, B - 1)),
    ]
    new, hartree = pl.pallas_call(
        functools.partial(kernel, (A, B, C, doms, planes, ny, nz)),
        out_shape=(
            jax.ShapeDtypeStruct(orbitals.shape, f32),
            jax.ShapeDtypeStruct((planes, rows_own, nz), f32),
        ),
        in_specs=[pl.BlockSpec(memory_space=pltpu.SMEM)] + [hbm] * 5,
        out_specs=(hbm, vmem),
        scratch_shapes=scratch,
        compiler_params=pltpu.CompilerParams(
            collective_id=0, has_side_effects=True, vmem_limit_bytes=60 * 2**20
        ),
    )(
        occupations,
        orbitals,
        potential,
        jnp.asarray(np.concatenate([dz, dz], axis=0), jnp.bfloat16),
        jnp.asarray(np.concatenate([dy, dy], axis=1), jnp.bfloat16),
        jnp.asarray(table),
    )
    return pl.pallas_call(
        finish_kernel,
        out_shape=(
            jax.ShapeDtypeStruct(orbitals.shape, f32),
            jax.ShapeDtypeStruct((planes, rows_own, nz), f32),
        ),
        in_specs=[hbm] * 2,
        out_specs=(hbm, hbm),
        scratch_shapes=[
            pltpu.VMEM(orbitals.shape[1:], f32),
            pltpu.VMEM((planes, rows_own, nz), f32),
            dma((2, 9)),
        ],
        compiler_params=pltpu.CompilerParams(vmem_limit_bytes=60 * 2**20),
    )(new, hartree)


def solution(mesh):
    return jax.shard_map(
        body,
        mesh=mesh,
        in_specs=(P("orb", None, "dom", None, None), P("orb"), P("dom", None, None)),
        out_specs=(P("orb", None, "dom", None, None), P("dom", "orb", None)),
        check_vma=False,
    )
```

```python
import functools
import math

import jax
import jax.numpy as jnp
import numpy as np
from jax import lax
from jax.experimental import pallas as pl
from jax.experimental.pallas import tpu as pltpu
from jax.sharding import PartitionSpec as P

MESH = pl.DeviceIdType.MESH
HIGHEST = lax.Precision.HIGHEST
SPACING = 0.4
TIME_STEP = 0.03
STENCIL = (-205.0 / 72.0, 8.0 / 5.0, -1.0 / 5.0, 8.0 / 315.0, -1.0 / 560.0)
COEF = tuple(-0.5 * c / (SPACING * SPACING) for c in STENCIL)


def real_basis(n):
    grid = np.arange(n)
    rows = np.zeros((n, n))
    for k in range(n):
        m = (k + 1) // 2
        angle = 2.0 * np.pi * ((m * grid) % n) / n
        wave = np.cos(angle) if (k % 2 == 1 or k == 0) else np.sin(angle)
        rows[k] = wave * (np.sqrt(1.0 / n) if m in (0, n // 2) else np.sqrt(2.0 / n))
    return rows


def band(n):
    out = np.zeros((n, n))
    for r in range(1, 5):
        out += COEF[r] * (np.eye(n, k=r) + np.eye(n, k=-r))
    return out


def squares_of(n):
    m = (np.arange(n) + 1) // 2
    return (m * (2.0 * math.pi / (n * SPACING))) ** 2


def dot(a, b):
    return jnp.dot(a, b, precision=HIGHEST, preferred_element_type=jnp.float32)


def wrap(value, n):
    return jnp.where(value >= n, value - n, value)


def layout(nx, ny, nz):
    rows, places = 0, {}
    for name, count in (
        ("wy0", ny),
        ("wy1", ny),
        ("iy0", ny),
        ("iy1", ny),
        ("rz", nz),
        ("rzt", nz),
        ("rx", nx),
        ("rxt", nx),
        ("qx", nx),
        ("qz", 8),
    ):
        places[name] = (rows, count)
        rows += -(-count // 8) * 8
    return places, rows


def kernel(
    dims,
    occ_ref,
    orb_ref,
    pot_hbm,
    dz_hbm,
    dy_hbm,
    table_hbm,
    new_ref,
    out_ref,
    buf,
    res,
    pot_ref,
    dz_ref,
    dy_ref,
    tab,
    m1,
    r1,
    s1,
    r2,
    s2,
    r3,
    xs,
    y3,
    r4,
    m5,
    r5,
    s5,
    r6,
    load,
    store,
    token,
    send0,
    recv0,
    send1,
    recv1,
    send2,
    recv2,
    send3,
    recv3,
    send4,
    recv4,
    send5,
    recv5,
    send6,
    recv6,
):
    A, B, C, D, planes, ny, nz = dims
    nx = planes * D
    half = planes // 2
    groups = B * C
    keep = ny // groups
    rows_a = ny // A
    rows_own = ny // (A * groups)
    line = A * D
    stride = line // keep
    last = 4 + planes
    places, _ = layout(nx, ny, nz)

    orb = lax.axis_index("orb")
    dom = lax.axis_index("dom")
    a = orb // groups
    b = lax.rem(orb // C, B)
    c = lax.rem(orb, C)
    inner = orb - a * groups
    me = a * D + dom
    odd = lax.rem(dom, 2)
    fast_id = dom + 1 - 2 * odd
    slow_id = dom - 1 + 2 * odd
    has_slow = jnp.logical_and(slow_id >= 0, slow_id < D)
    base_fast = (1 - odd) * (planes - 4)
    base_slow = odd * (planes - 4)
    size = (B, C)
    mine = (b, c)

    def along(axis, offset):
        if axis == 0:
            return {"orb": a * groups + wrap(b + offset, B) * C + c}
        return {"orb": a * groups + b * C + wrap(c + offset, C)}

    def on_line(offset):
        slab = dom + offset % D
        over = (slab >= D).astype(jnp.int32)
        slab = slab - D * over
        block = wrap(a + offset // D + over, A)
        return {"orb": block * groups + inner, "dom": slab}, block * D + slab, slab

    barrier = pltpu.get_barrier_semaphore()
    for offset in (1, line - 1):
        pl.semaphore_signal(barrier, inc=1, device_id=on_line(offset)[0], device_id_type=MESH)
    for axis in range(2):
        for o in range(1, size[axis]):
            pl.semaphore_signal(barrier, inc=1, device_id=along(axis, o), device_id_type=MESH)
    loads = [
        pltpu.make_async_copy(orb_ref.at[0, 0], buf.at[0, 0, pl.ds(4, planes)], load.at[0]),
        pltpu.make_async_copy(orb_ref.at[0, 1], buf.at[0, 1, pl.ds(4, planes)], load.at[1]),
        pltpu.make_async_copy(dz_hbm, dz_ref, load.at[2]),
        pltpu.make_async_copy(dy_hbm, dy_ref, load.at[3]),
        pltpu.make_async_copy(pot_hbm, pot_ref, load.at[4]),
        pltpu.make_async_copy(table_hbm, tab, load.at[5]),
    ]
    for copy in loads:
        copy.start()
    pl.semaphore_wait(barrier, B + C)

    def halo(k, ch, side):
        base = base_slow if side else base_fast
        dst = jnp.where(odd == (0 if side else 1), last, 0)
        if k == 0:
            src = orb_ref.at[0, ch, pl.ds(base, 4)]
        else:
            src = buf.at[k, ch, pl.ds(4 + base, 4)]
        return pltpu.make_async_remote_copy(
            src_ref=src,
            dst_ref=buf.at[k, ch, pl.ds(dst, 4)],
            send_sem=send0.at[k, ch, side],
            recv_sem=recv0.at[k, ch, side],
            device_id={"dom": slow_id if side else fast_id},
            device_id_type=MESH,
        )

    def guarded(side, act):
        if side:
            pl.when(has_slow)(act)
        else:
            act()

    def start(k, ch, side):
        guarded(side, lambda: halo(k, ch, side).start())

    def arrived(k, ch, side):
        guarded(side, lambda: halo(k, ch, side).wait_recv())

    for ch in range(2):
        start(0, ch, 1)
    for ch in range(2):
        start(0, ch, 0)

    def tell(r):
        reach = 2**r
        for offset in (reach, line - reach):
            pl.semaphore_signal(token.at[r], inc=1, device_id=on_line(offset)[0], device_id_type=MESH)

    def told(r):
        pl.semaphore_wait(token.at[r], 2)

    rounds = max(1, (line // 2).bit_length() - 1)
    tell(0)

    @pl.when(jnp.logical_not(has_slow))
    def _():
        edge = odd * last
        for k in range(3):
            for ch in range(2):
                buf[k, ch, pl.ds(edge, 4)] = jnp.zeros((4, ny, nz), jnp.float32)

    def step(k, ch, x):
        f = buf[k, ch, 4 + x]
        high = f.astype(jnp.bfloat16)
        low = (f - high.astype(jnp.float32)).astype(jnp.bfloat16)
        h = jnp.dot(jnp.concatenate([high, low], axis=1), dz_ref[...], preferred_element_type=jnp.float32)
        h = h + jnp.dot(dy_ref[...], jnp.concatenate([high, low], axis=0), preferred_element_type=jnp.float32)
        h = h + (3.0 * COEF[0] + pot_ref[x]) * f
        for r in range(1, 5):
            h = h + COEF[r] * (buf[k, ch, 4 + x + r] + buf[k, ch, 4 + x - r])
        sign = 1.0 if (k + ch) % 2 else -1.0
        return (sign * TIME_STEP / (k + 1)) * h

    weight = occ_ref[0] * (1.0 / math.sqrt(A * groups))

    def sweep(k, ch, base):
        def body(i, carry):
            x = base + i
            out = step(k, ch, x)
            if k < 2:
                buf[k + 1, ch, 4 + x] = out
            elif ch == 0:
                res[1, x] = ((buf[0, 1, 4 + x] + buf[1, 0, 4 + x]) + buf[2, 1, 4 + x]) + out
            else:
                real = ((buf[0, 0, 4 + x] + buf[1, 1, 4 + x]) + buf[2, 0, 4 + x]) + out
                res[0, x] = real
                imag = res[1, x]
                m1[i // 2, base // 2 + lax.rem(i, 2)] = weight * (real * real + imag * imag)
            return carry

        lax.fori_loop(0, 4, body, 0, unroll=4)
        if k == 2 and ch == 1:
            for h in range(2):
                first, count = places["wy%d" % h]
                for i in range(2):
                    at = base // 2 + i
                    m1[h, at] = dot(tab[first : first + count, :ny], m1[h, at])

    def middle(k, ch):
        for base in range(4, planes - 4, 4):
            sweep(k, ch, base)

    def edge_of(k, ch, side):
        arrived(k, ch, side)
        sweep(k, ch, base_slow if side else base_fast)
        if k < 2:
            start(k + 1, ch, side)

    loads[2].wait()
    loads[3].wait()
    loads[4].wait()
    for ch in range(2):
        loads[ch].wait()
        middle(0, ch)
    for ch in range(2):
        edge_of(0, ch, 0)
    told(0)
    if rounds > 1:
        tell(1)
    edge_of(0, 0, 1)
    middle(1, 0)
    edge_of(1, 0, 0)
    edge_of(0, 1, 1)
    middle(1, 1)
    edge_of(1, 1, 0)
    if rounds > 1:
        told(1)
    if rounds > 2:
        tell(2)
    edge_of(1, 0, 1)
    middle(2, 0)
    edge_of(2, 0, 0)
    edge_of(1, 1, 1)
    loads[5].wait()
    middle(2, 1)
    edge_of(2, 1, 0)

    early = planes // 2 - 2
    starts = ((1 - odd) * 2, odd * early)
    counts = (early, 2)

    def first_hop(t, h, o):
        axis = h
        big = ny // size[axis]
        peer = wrap(mine[axis] + o, size[axis])
        part = pl.ds(starts[t], counts[t])
        return pltpu.make_async_remote_copy(
            src_ref=m1.at[h, part, pl.ds(pl.multiple_of(peer * big, 8), big)],
            dst_ref=r1.at[h, o - 1, part],
            send_sem=send1.at[t, h, o - 1],
            recv_sem=recv1.at[t, h, o - 1],
            device_id=along(axis, o),
            device_id_type=MESH,
        )

    def second_hop(t, h, o):
        axis = 1 - h
        peer = wrap(mine[axis] + o, size[axis])
        part = pl.ds(starts[t], counts[t])
        return pltpu.make_async_remote_copy(
            src_ref=s1.at[h, part, pl.ds(pl.multiple_of(peer * keep, 8), keep)],
            dst_ref=r2.at[h, o - 1, part],
            send_sem=send2.at[t, h, o - 1],
            recv_sem=recv2.at[t, h, o - 1],
            device_id=along(axis, o),
            device_id_type=MESH,
        )

    def offsets(n):
        return sorted(range(1, n), key=lambda o: -min(o, n - o))

    def each(t, make, act):
        for h in range(2):
            axis = h if make in (first_hop, third_hop) else 1 - h
            for o in offsets(size[axis]):
                act(make(t, h, o))

    def begin(copy):
        copy.start()

    def left(copy):
        copy.wait_send()

    def third_hop(t, h, o):
        axis = h
        big = rows_a // size[axis]
        peer = wrap(mine[axis] + o, size[axis])
        return pltpu.make_async_remote_copy(
            src_ref=m5.at[h, :, pl.ds(pl.multiple_of(a * rows_a + peer * big, 8), big)],
            dst_ref=r5.at[h, o - 1],
            send_sem=send5.at[h, o - 1],
            recv_sem=recv5.at[h, o - 1],
            device_id=along(axis, o),
            device_id_type=MESH,
        )

    def fourth_hop(t, h, o):
        axis = 1 - h
        peer = wrap(mine[axis] + o, size[axis])
        return pltpu.make_async_remote_copy(
            src_ref=s5.at[h, peer],
            dst_ref=r6.at[h, o - 1],
            send_sem=send6.at[h, o - 1],
            recv_sem=recv6.at[h, o - 1],
            device_id=along(axis, o),
            device_id_type=MESH,
        )

    each(0, first_hop, begin)
    if rounds > 2:
        told(2)
    if rounds > 3:
        tell(3)
    edge_of(2, 0, 1)
    pltpu.make_async_copy(res.at[1], new_ref.at[0, 1], store.at[1]).start()
    edge_of(2, 1, 1)
    each(1, first_hop, begin)
    pltpu.make_async_copy(res.at[0], new_ref.at[0, 0], store.at[0]).start()
    for t in range(2):
        part = pl.ds(starts[t], counts[t])
        for h in range(2):
            axis = h
            big = ny // size[axis]
            total = m1[h, part, pl.ds(pl.multiple_of(mine[axis] * big, 8), big)]
            for o in range(1, size[axis]):
                first_hop(t, h, o).wait_recv()
                total = total + r1[h, o - 1, part]
            s1[h, part] = total
            for o in offsets(size[1 - h]):
                second_hop(t, h, o).start()
    each(0, second_hop, lambda copy: copy.wait_recv())
    each(1, second_hop, lambda copy: copy.wait_recv())
    for h in range(2):
        axis = 1 - h
        total = s1[h, :, pl.ds(pl.multiple_of(mine[axis] * keep, 8), keep)]
        for o in range(1, size[axis]):
            total = total + r2[h, o - 1]
        for p in range(half):
            s2[:, (p // 2) * 4 + 2 * h + p % 2, :] = total[p]

    if rounds > 3:
        told(3)
    here = me // stride
    spot = lax.rem(me, stride)
    second = spot == stride // 2
    solver = jnp.logical_or(spot == 0, second)
    own = jnp.where(second, wrap(here + keep // 2, keep), here)

    def to_solver(s, i):
        j = wrap(here + i, keep)
        place = j * stride if s == 0 else wrap(j + keep // 2, keep) * stride + stride // 2
        block = place // D
        return pltpu.make_async_remote_copy(
            src_ref=s2.at[j],
            dst_ref=r3.at[me],
            send_sem=send3.at[s, i],
            recv_sem=recv3.at[me],
            device_id={"orb": block * groups + inner, "dom": place - block * D},
            device_id_type=MESH,
        )

    def to_solvers(act):
        for far in range(keep // 2, -1, -1):
            for s in range(2):
                for step_ in sorted({far, (keep - far) % keep}):
                    i = (step_ + s * (keep // 2)) % keep
                    if far:
                        act(to_solver(s, i))
                    else:
                        pl.when(spot != s * (stride // 2))(lambda s=s, i=i: act(to_solver(s, i)))

    to_solvers(begin)

    def to_slab(offset):
        place = lax.rem(me + offset + line - jnp.where(second, stride // 2, 0), line)
        block = place // D
        slab = place - block * D
        copy = pltpu.make_async_remote_copy(
            src_ref=y3.at[slab],
            dst_ref=r4.at[own],
            send_sem=send4.at[offset + line // 4],
            recv_sem=recv4.at[own],
            device_id={"orb": block * groups + inner, "dom": slab},
            device_id_type=MESH,
        )
        return copy, place != me

    far_first = sorted(range(-(line // 4), line // 4), key=lambda o: -abs(o))

    def to_slabs(act):
        for offset in far_first:
            copy, other = to_slab(offset)
            pl.when(other)(lambda copy=copy: act(copy))

    @pl.when(solver)
    def _():
        r3[me] = s2[own]
        for offset in range(1, line):
            device, place, slab = on_line(offset)
            pltpu.make_async_remote_copy(
                src_ref=s2.at[0],
                dst_ref=r3.at[place],
                send_sem=send3.at[0, 0],
                recv_sem=recv3.at[place],
                device_id=device,
                device_id_type=MESH,
            ).wait_recv()
        for slab in range(D):
            piece = r3[slab]
            for q in range(1, A):
                piece = piece + r3[q * D + slab]
            xs[slab * planes : (slab + 1) * planes, :] = piece

        def table(name):
            first, count = places[name]
            return tab[first : first + count, :]

        modes = dot(table("rx")[:, :nx], dot(xs[...], table("rzt")))
        wave = inner * keep + own
        m = ((wave + 1) // 2).astype(jnp.float32) * (2.0 * math.pi / (ny * SPACING))
        squares = (table("qx") + m * m) + table("qz")[:1]
        positive = squares > 0.0
        solved = modes * jnp.where(positive, 4.0 * math.pi / jnp.where(positive, squares, 1.0), 0.0)
        xs[...] = dot(dot(table("rxt")[:, :nx], solved), table("rz"))
        for slab in range(D):
            y3[slab] = xs[slab * planes : (slab + 1) * planes, :]
        to_slabs(begin)
        r4[own] = y3[dom]

    def from_solver(i):
        j = wrap(own + i, keep)
        place = j * stride
        block = place // D
        return pltpu.make_async_remote_copy(
            src_ref=y3.at[0],
            dst_ref=r4.at[j],
            send_sem=send4.at[0],
            recv_sem=recv4.at[j],
            device_id={"orb": block * groups + inner, "dom": place - block * D},
            device_id_type=MESH,
        )

    for i in range(1, keep):
        from_solver(i).wait_recv()

    @pl.when(jnp.logical_not(solver))
    def _():
        from_solver(0).wait_recv()

    for h in range(2):
        table = tab[pl.ds(pl.multiple_of(places["iy%d" % h][0] + inner * keep, 8), keep), :]
        for p in range(half):
            rows = r4[:, (p // 2) * 4 + 2 * h + p % 2, :]
            m5[h, p] = lax.dot_general(
                table, rows, (((0,), (0,)), ((), ())), precision=HIGHEST, preferred_element_type=jnp.float32
            )[:ny]
        for o in offsets(size[h]):
            third_hop(0, h, o).start()
    for h in range(2):
        axis = h
        big = rows_a // size[axis]
        total = m5[h, :, pl.ds(pl.multiple_of(a * rows_a + mine[axis] * big, 8), big)]
        for o in range(1, size[axis]):
            third_hop(0, h, o).wait_recv()
            total = total + r5[h, o - 1]
        for p in range(size[1 - h]):
            s5[h, p] = total[:, p * rows_own : (p + 1) * rows_own]
        for o in offsets(size[1 - h]):
            fourth_hop(0, h, o).start()
    for h in range(2):
        axis = 1 - h
        total = s5[h, mine[axis]]
        for o in range(1, size[axis]):
            fourth_hop(0, h, o).wait_recv()
            total = total + r6[h, o - 1]
        for p in range(half):
            out_ref[(p // 2) * 4 + 2 * h + p % 2] = total[p]

    for k in range(3):
        for ch in range(2):
            for side in range(2):
                guarded(side, lambda k=k, ch=ch, side=side: halo(k, ch, side).wait_send())
    for t in range(2):
        each(t, first_hop, left)
        each(t, second_hop, left)
    each(0, third_hop, left)
    each(0, fourth_hop, left)
    to_solvers(left)

    @pl.when(solver)
    def _():
        to_slabs(left)

    for part in range(2):
        pltpu.make_async_copy(res.at[part], new_ref.at[0, part], store.at[part]).wait()


def finish_kernel(new_in, out_in, new_ref, out_ref, held, small, sems):
    cut = new_in.shape[2] // 4
    pieces = [(part, pl.ds(q * cut, cut)) for part in range(2) for q in range(4)]
    count = len(pieces)
    ins = [
        pltpu.make_async_copy(new_in.at[0, part, piece], held.at[part, piece], sems.at[0, i])
        for i, (part, piece) in enumerate(pieces)
    ]
    outs = [
        pltpu.make_async_copy(held.at[part, piece], new_ref.at[0, part, piece], sems.at[1, i])
        for i, (part, piece) in enumerate(pieces)
    ]
    ins.append(pltpu.make_async_copy(out_in, small, sems.at[0, count]))
    outs.append(pltpu.make_async_copy(small, out_ref, sems.at[1, count]))
    for copy in ins:
        copy.start()
    for first, second in zip(ins, outs):
        first.wait()
        second.start()
    for copy in outs:
        copy.wait()


def factors(orbs):
    return {64: (4, 4, 4), 8: (2, 2, 2)}[orbs]


def body(orbitals, occupations, potential):
    groups = lax.axis_size("orb")
    doms = lax.axis_size("dom")
    A, B, C = factors(groups)
    planes, ny, nz = potential.shape
    nx = planes * doms
    half = planes // 2
    keep = ny // (B * C)
    rows_own = ny // groups
    line = A * doms
    f32 = jnp.float32
    vmem = pl.BlockSpec(memory_space=pltpu.VMEM)
    hbm = pl.BlockSpec(memory_space=pltpu.HBM)
    dma = pltpu.SemaphoreType.DMA

    dz = band(nz)
    dy = band(ny)
    ry = real_basis(ny)
    rz = real_basis(nz)
    rx = real_basis(nx)
    swapped = ry.reshape(B, C, keep, ny).transpose(1, 0, 2, 3).reshape(ny, ny)
    back = ry.reshape(ny, A, B, C, rows_own).transpose(0, 1, 3, 2, 4).reshape(ny, ny)
    places, rows = layout(nx, ny, nz)
    table = np.zeros((rows, max(ny, nz, nx)), np.float32)
    for name, value in (
        ("wy0", ry),
        ("wy1", swapped),
        ("iy0", ry),
        ("iy1", back),
        ("rz", rz),
        ("rzt", rz.T),
        ("rx", rx),
        ("rxt", rx.T),
        ("qx", squares_of(nx)[:, None] * np.ones((1, nz))),
        ("qz", squares_of(nz)[None, :]),
    ):
        first = places[name][0]
        table[first : first + value.shape[0], : value.shape[1]] = value
    scratch = [
        pltpu.VMEM((3, 2, planes + 8, ny, nz), f32),
        pltpu.VMEM((2, planes, ny, nz), f32),
        pltpu.VMEM((planes, ny, nz), f32),
        pltpu.VMEM((2 * nz, nz), jnp.bfloat16),
        pltpu.VMEM((ny, 2 * ny), jnp.bfloat16),
        pltpu.VMEM(table.shape, f32),
        pltpu.VMEM((2, half, ny, nz), f32),
        pltpu.VMEM((2, B - 1, half, ny // B, nz), f32),
        pltpu.VMEM((2, half, ny // B, nz), f32),
        pltpu.VMEM((2, B - 1, half, keep, nz), f32),
        pltpu.VMEM((keep, planes, nz), f32),
        pltpu.VMEM((line, planes, nz), f32),
        pltpu.VMEM((nx, nz), f32),
        pltpu.VMEM((doms, planes, nz), f32),
        pltpu.VMEM((keep, planes, nz), f32),
        pltpu.VMEM((2, half, ny, nz), f32),
        pltpu.VMEM((2, B - 1, half, ny // (A * B), nz), f32),
        pltpu.VMEM((2, B, half, rows_own, nz), f32),
        pltpu.VMEM((2, B - 1, half, rows_own, nz), f32),
        dma((6,)),
        dma((2,)),
        pltpu.SemaphoreType.REGULAR((4,)),
        dma((3, 2, 2)),
        dma((3, 2, 2)),
        dma((2, 2, B - 1)),
        dma((2, 2, B - 1)),
        dma((2, 2, B - 1)),
        dma((2, 2, B - 1)),
        dma((2, keep)),
        dma((line,)),
        dma((line // 2,)),
        dma((keep,)),
        dma((2, B - 1)),
        dma((2, B - 1)),
        dma((2, B - 1)),
        dma((2, B - 1)),
    ]
    new, hartree = pl.pallas_call(
        functools.partial(kernel, (A, B, C, doms, planes, ny, nz)),
        out_shape=(
            jax.ShapeDtypeStruct(orbitals.shape, f32),
            jax.ShapeDtypeStruct((planes, rows_own, nz), f32),
        ),
        in_specs=[pl.BlockSpec(memory_space=pltpu.SMEM)] + [hbm] * 5,
        out_specs=(hbm, vmem),
        scratch_shapes=scratch,
        compiler_params=pltpu.CompilerParams(
            collective_id=0, has_side_effects=True, vmem_limit_bytes=60 * 2**20
        ),
    )(
        occupations,
        orbitals,
        potential,
        jnp.asarray(np.concatenate([dz, dz], axis=0), jnp.bfloat16),
        jnp.asarray(np.concatenate([dy, dy], axis=1), jnp.bfloat16),
        jnp.asarray(table),
    )
    return pl.pallas_call(
        finish_kernel,
        out_shape=(
            jax.ShapeDtypeStruct(orbitals.shape, f32),
            jax.ShapeDtypeStruct((planes, rows_own, nz), f32),
        ),
        in_specs=[hbm] * 2,
        out_specs=(hbm, hbm),
        scratch_shapes=[
            pltpu.VMEM(orbitals.shape[1:], f32),
            pltpu.VMEM((planes, rows_own, nz), f32),
            dma((2, 9)),
        ],
        compiler_params=pltpu.CompilerParams(vmem_limit_bytes=60 * 2**20),
    )(new, hartree)


def solution(mesh):
    return jax.shard_map(
        body,
        mesh=mesh,
        in_specs=(P("orb", None, "dom", None, None), P("orb"), P("dom", None, None)),
        out_specs=(P("orb", None, "dom", None, None), P("dom", "orb", None)),
        check_vma=False,
    )
```
